256 devices in a mesh: sec: 4 (over x), ch: 64 (over y, z, core).
Axes of the slice: x: 4, y: 4, z: 8, core: 2. Of those that a mesh axis runs over, the one named last changes fastest.
Arguments:
- strain_rate: bfloat16 [4, 32768, 4156], P(None, ('sec', 'ch')), may hold values from -60 to 60
- fir_taps: bfloat16 [64], replicated, may hold values from -0.75 to 0.75
- gain_code: int32 [32768], P(('sec', 'ch')), may hold values from 1 to 8
- alive_mask: int32 [32768], P(('sec', 'ch')), may hold values 0 or 1
- band_low: int32 [1], replicated, may hold values from 1 to 255
- band_high: int32 [1], replicated, may hold values from 256 to 510
- slow_limit: int32 [1], replicated, may hold values from 200 to 599
- fast_limit: int32 [1], replicated, may hold values from 1500 to 4999
Outputs:
- filtered: float32 [4, 32768, 1024], P('sec', 'ch')
The draws below stay inside these ranges and needn't reach their ends.
All inputs are finite; a program needn't handle non-finite values. No bound on the sum of `alive_mask` on one device may be relied on, other than what follows from the above.
Results may differ from the reference program's by a relative error of at most 0.0003.
Values sent between devices are 32-bit elements; how exact they have to be, the bound alone decides.
A program may use at most 128 MiB of HBM per device.

```python
import math
import jax
import jax.numpy as jnp
from jax import lax

DECIMATED_COUNT = 1024
BINS = 512
TAPS = 64
DECIM = 4
SMOOTH = 4
WINDOWS = 4
CHANNELS = 32768
RAW = 4156
RATE = 16000


def draw_strain_rate(key, part):
    noise_key = jax.random.fold_in(key, 0)
    scale_key = jax.random.fold_in(key, 1)
    quiet_key = jax.random.fold_in(key, 3)
    pick_key = jax.random.fold_in(key, 4)
    shape = (WINDOWS, CHANNELS, RAW)
    channel_scale = jnp.exp(jax.random.uniform(scale_key, (1, CHANNELS, 1), jnp.float32, 0.0, math.log(10.0)))
    quiet_draw = jax.random.randint(quiet_key, (CHANNELS,), 0, 48)
    quiet_pick = jax.random.randint(pick_key, (), 0, CHANNELS)
    channel_number = jnp.arange(CHANNELS, dtype=jnp.int32)
    quiet = (quiet_draw == 0) | (channel_number == quiet_pick)
    quiet_factor = jnp.where(quiet, 0.001, 1.0).astype(jnp.float32)[None, :, None]
    channel_scale = channel_scale * quiet_factor
    values = jax.random.truncated_normal(noise_key, -6.0, 6.0, shape, jnp.float32) * channel_scale
    return values.astype(jnp.bfloat16)


def set_ends(array, own_key, low, largest):
    extent = array.shape
    spot = [jax.random.randint(jax.random.fold_in(own_key, axis), (), 0, extent[axis]) for axis in range(len(extent))]
    array = array.at[tuple(spot)].set(low)
    longest = extent.index(max(extent))
    spot[longest] = (spot[longest] + 1) % extent[longest]
    return array.at[tuple(spot)].set(largest)


def bell_draw(key, extent, width, limit, kind=jnp.bfloat16):
    return jnp.clip(width * jax.random.normal(key, extent, jnp.float32), -limit, limit).astype(kind)


def setup_inputs(seed: int = 0) -> dict:
    seeds = jax.random.split(jax.random.key(seed), 9)
    return {
        "strain_rate": draw_strain_rate(jax.random.fold_in(seeds[8], 71), 0),
        "fir_taps": bell_draw(seeds[1], (TAPS,), TAPS ** -0.5, 0.75),
        "gain_code": set_ends(jax.random.randint(seeds[2], (CHANNELS,), 1, 9), jax.random.fold_in(seeds[2], 1), 1, 8).astype(jnp.int32),
        "alive_mask": set_ends((jax.random.randint(seeds[3], (CHANNELS,), 0, 16) < 15).astype(jnp.int32), jax.random.fold_in(seeds[3], 1), 0, 1),
        "band_low": jax.random.randint(seeds[4], (1,), 1, BINS // 2).astype(jnp.int32),
        "band_high": jax.random.randint(seeds[5], (1,), BINS // 2, BINS - 1).astype(jnp.int32),
        "slow_limit": jax.random.randint(seeds[6], (1,), 200, 600).astype(jnp.int32),
        "fast_limit": jax.random.randint(seeds[7], (1,), 1500, 5000).astype(jnp.int32),
    }


FLOOR = 0.05

def decimate(window, fir_taps):
    channels = window.shape[0]
    phases = window.astype(jnp.float32).reshape(channels, DECIMATED_COUNT + (TAPS - DECIM) // DECIM, DECIM)
    weights = fir_taps.astype(jnp.float32).reshape(TAPS // DECIM, DECIM)
    total = jnp.zeros((channels, DECIMATED_COUNT), jnp.float32)
    for offset in range(TAPS // DECIM):
        piece = phases[:, offset:offset + DECIMATED_COUNT, :].reshape(channels * DECIMATED_COUNT, DECIM)
        total = total + jnp.dot(piece, weights[offset], preferred_element_type=jnp.float32).reshape(channels, DECIMATED_COUNT)
    return total

def reference(strain_rate, fir_taps, gain_code, alive_mask, band_low, band_high, slow_limit, fast_limit):
    bin_index = jnp.arange(BINS, dtype=jnp.int32)
    band = ((bin_index >= band_low[0]) & (bin_index <= band_high[0])).astype(jnp.float32)
    weight = gain_code.astype(jnp.float32) * 0.25 * alive_mask.astype(jnp.float32)
    wave_index = jnp.arange(CHANNELS, dtype=jnp.int32)
    channel_spacing = jnp.minimum(wave_index, CHANNELS - wave_index)
    reach = bin_index * RATE
    fan = ((slow_limit[0] * channel_spacing[:, None] <= reach[None, :]) & (reach[None, :] <= fast_limit[0] * channel_spacing[:, None])).astype(jnp.int32)
    fan_float = fan.astype(jnp.float32)

    def one_window(window):
        downsampled_traces = decimate(window, fir_taps)
        frequency_content = jnp.fft.rfft(downsampled_traces, axis=1)[:, :BINS] / math.sqrt(DECIMATED_COUNT)
        real_part = jnp.real(frequency_content)
        imag_part = jnp.imag(frequency_content)
        amplitude = jnp.sqrt(real_part * real_part + imag_part * imag_part)
        padded = jnp.pad(amplitude, ((0, 0), (SMOOTH, SMOOTH)))
        total = padded[:, 0:BINS]
        for shift in range(1, 2 * SMOOTH + 1):
            total = total + padded[:, shift:shift + BINS]
        smooth = total / (2 * SMOOTH + 1)
        factor = band[None, :] * weight[:, None] / jnp.maximum(smooth, FLOOR)
        whitened = lax.complex(real_part * factor, imag_part * factor)
        wavefield = jnp.fft.fft(whitened, axis=0)
        passed = jnp.fft.ifft(wavefield * fan_float, axis=0)
        full = jnp.pad(passed, ((0, 0), (0, DECIMATED_COUNT - BINS)))
        return 2.0 * math.sqrt(DECIMATED_COUNT) * jnp.real(jnp.fft.ifft(full, axis=1))
    return lax.map(one_window, strain_rate)
```

```python
import functools
import math

import jax
import jax.numpy as jnp
import ml_dtypes
import numpy as np
from jax import lax
from jax.experimental import pallas as pl
from jax.experimental.pallas import tpu as pltpu
from jax.sharding import PartitionSpec as P

TAPS = 64
DECIM = 4
SMOOTH = 4
FLOOR = 0.05
SAMPLES = 1024
BINS = 512
PAD = 16
ALIGN = 16
OUT = 128
SPAN = DECIM * OUT
INNER = 128
OUTER = 256
SECTIONS = 4
SHARDS = 64
TABLE_ROWS = PAD + BINS + PAD
VARIANTS = (8,)
VMEM_LIMIT = 48 * 1024 * 1024
MESH = pl.DeviceIdType.MESH
VM = pltpu.VMEM
SM = pltpu.SMEM


def split_np(table):
    table = table.astype(np.float32)
    high = table.astype(ml_dtypes.bfloat16)
    low = (table - high.astype(np.float32)).astype(ml_dtypes.bfloat16)
    return high, low


def split(value):
    high = value.astype(jnp.bfloat16)
    low = (value - high.astype(jnp.float32)).astype(jnp.bfloat16)
    return high, low


def mm(a, b):
    return jnp.dot(a, b, preferred_element_type=jnp.float32)


def mm_nt(a, b):
    return lax.dot_general(a, b, (((1,), (1,)), ((), ())), preferred_element_type=jnp.float32)


def time_tables():
    f = np.arange(BINS)[:, None]
    t = np.arange(SAMPLES)[None, :]
    angle = (f * t % SAMPLES) * (2.0 * math.pi / SAMPLES)
    table = np.zeros((2, TABLE_ROWS, SAMPLES))
    table[0, PAD : PAD + BINS] = np.cos(angle) / 32.0
    table[1, PAD : PAD + BINS] = -np.sin(angle) / 32.0
    return split_np(table)


def wave_tables():
    k = np.arange(OUTER)
    angle = (k[:, None] * k[None, :] % OUTER) * (2.0 * math.pi / OUTER)
    c, s = np.cos(angle), np.sin(angle)
    outer = split_np(np.block([[c, s], [-s, c]]))
    outer_back = split_np(np.block([[c, -s], [s, c]]) / (OUTER * INNER))
    j = np.arange(INNER)
    angle = (j[:, None] * j[None, :] % INNER) * (2.0 * math.pi / INNER)
    c, s = np.cos(angle), np.sin(angle)
    inner = split_np(np.block([[c, -s], [s, c]]))
    inner_back = split_np(np.block([[c, s], [-s, c]]))
    angle = k[:, None] * j[None, :] * (2.0 * math.pi / (OUTER * INNER))
    twist = np.stack([np.cos(angle), np.sin(angle)]).astype(np.float32)
    return outer, outer_back, inner, inner_back, twist


def first_bin(scal, nb):
    return jnp.minimum(scal[0], BINS - nb * SHARDS)


def front_kernel(
    nb, scal, strain, taps, weight, table_h, table_l, s_ref, dec, amp, parts
):
    rows = nb * SHARDS
    wide = rows + 2 * PAD
    f0 = pl.multiple_of(first_bin(scal, nb), ALIGN)
    fir = jnp.broadcast_to(taps[...], (OUT, taps.shape[1]))
    fir = pltpu.roll(fir, 0, 1, stride=DECIM, stride_axis=0).astype(jnp.bfloat16)
    tail = SPAN + TAPS - DECIM
    index = f0 + lax.broadcasted_iota(jnp.int32, (rows, INNER), 0)
    band = ((index >= scal[1]) & (index <= scal[2])).astype(jnp.float32)
    scale = band * weight[...]

    def pair(p, carry):
        for w in range(2):
            for q in range(SAMPLES // OUT):
                size = SPAN + OUT if (q + 1) * SPAN + OUT <= strain.shape[2] else tail
                piece = strain[2 * p + w, :, q * SPAN : q * SPAN + size]
                dec[w * INNER : (w + 1) * INNER, q * OUT : (q + 1) * OUT] = mm_nt(
                    piece, fir[:, :size]
                )
        high, low = split(dec[...])
        for part in range(2):
            th = table_h[part, pl.ds(f0, wide), :]
            tl = table_l[part, pl.ds(f0, wide), :]
            parts[part] = mm_nt(th, high) + mm_nt(th, low) + mm_nt(tl, high)
        real, imag = parts[0], parts[1]
        amp[...] = jnp.sqrt(real * real + imag * imag)
        total = amp[PAD - SMOOTH : PAD - SMOOTH + rows, :]
        for d in range(1, 2 * SMOOTH + 1):
            total = total + amp[PAD - SMOOTH + d : PAD - SMOOTH + d + rows, :]
        smooth = total / (2 * SMOOTH + 1)
        smooth = jnp.maximum(smooth, FLOOR)
        for w in range(2):
            lanes = slice(w * INNER, (w + 1) * INNER)
            factor = scale / smooth[:, lanes]
            start = pl.multiple_of((2 * p + w) * SHARDS, SHARDS)
            for part in range(2):
                value = parts[part, PAD : PAD + rows, lanes] * factor
                s_ref[part, :, pl.ds(start, SHARDS), :] = value.reshape(nb, SHARDS, INNER)
        return carry

    lax.fori_loop(0, SECTIONS // 2, pair, 0)


def wave_kernel(
    nb, chunks, scal, s_ref, outer_h, outer_l, back_h, back_l, in_h, in_l, inb_h, inb_l,
    twist, r_ref, x_ref, z_ref, fsend, frecv, bsend, brecv,
):
    sec = lax.axis_index("sec")
    ch = lax.axis_index("ch")
    y, z, core = ch // 16, (ch // 2) % 8, ch % 2
    me = sec * SHARDS + ch

    def each(action, with_sections):
        first = 16 if with_sections else 4

        def run(dz, dc, start):
            def step(q, carry):
                dx, dy = q // 4, q % 4
                to_ch = ((y + dy) % 4) * 16 + ((z + dz) % 8) * 2 + (core + dc) % 2
                action((sec + dx) % 4, to_ch)
                return carry

            lax.fori_loop(start, first, step, 0)

        for dz in (4, 3, 5, 2, 6, 1, 7):
            for dc in range(2):
                run(dz, dc, 0)
        run(0, 1, 0)
        run(0, 0, 1)

    barrier = pltpu.get_barrier_semaphore()
    each(
        lambda w, b: pl.semaphore_signal(
            barrier, inc=1, device_id=(w, b), device_id_type=MESH
        ),
        True,
    )
    pl.semaphore_wait(barrier, SECTIONS * SHARDS - 1)

    for n, (lo, size) in enumerate(chunks):
        bins = pl.ds(lo, size)
        pltpu.make_async_copy(
            s_ref.at[:, bins, pl.ds(me, 1)], x_ref.at[:, bins, pl.ds(me, 1)], frecv.at[n]
        ).start()

        def forward(w, b):
            pltpu.make_async_remote_copy(
                src_ref=s_ref.at[:, bins, pl.ds(w * SHARDS + b, 1)],
                dst_ref=x_ref.at[:, bins, pl.ds(me, 1)],
                send_sem=fsend.at[n],
                recv_sem=frecv.at[n],
                device_id=(w, b),
                device_id_type=MESH,
            ).start()

        each(forward, True)

    k1 = lax.broadcasted_iota(jnp.int32, (OUTER, INNER), 0)
    k2 = lax.broadcasted_iota(jnp.int32, (OUTER, INNER), 1)
    k = k1 + OUTER * k2
    spacing = jnp.minimum(k, OUTER * INNER - k)
    slow = scal[3] * spacing
    fast = scal[4] * spacing
    rate = 500 * OUTER * INNER // SAMPLES
    cosine, sine = twist[0], twist[1]

    def transform(jj, count):
        lanes = [slice(i * INNER, (i + 1) * INNER) for i in range(count)]
        field = jnp.concatenate(
            [
                jnp.concatenate([x_ref[part, jj + i] for i in range(count)], axis=1)
                for part in range(2)
            ],
            axis=0,
        )
        high, low = split(field)
        field = mm(outer_h[...], high) + mm(outer_h[...], low) + mm(outer_l[...], high)
        stacked = []
        for i in range(count):
            real, imag = field[:OUTER, lanes[i]], field[OUTER:, lanes[i]]
            stacked.append(
                jnp.concatenate(
                    [real * cosine + imag * sine, imag * cosine - real * sine], axis=1
                )
            )
        high, low = split(jnp.concatenate(stacked, axis=0))
        field = mm(high, in_h[...]) + mm(low, in_h[...]) + mm(high, in_l[...])
        masked = []
        for i in range(count):
            reach = (first_bin(scal, nb) + (jj + i) * SHARDS + ch) * rate
            fan = ((slow <= reach) & (reach <= fast)).astype(jnp.float32)
            block = field[i * OUTER : (i + 1) * OUTER]
            masked.append(
                jnp.concatenate([block[:, :INNER] * fan, block[:, INNER:] * fan], axis=1)
            )
        high, low = split(jnp.concatenate(masked, axis=0))
        field = mm(high, inb_h[...]) + mm(low, inb_h[...]) + mm(high, inb_l[...])
        reals, imags = [], []
        for i in range(count):
            block = field[i * OUTER : (i + 1) * OUTER]
            real, imag = block[:, :INNER], block[:, INNER:]
            reals.append(real * cosine - imag * sine)
            imags.append(imag * cosine + real * sine)
        field = jnp.concatenate(
            [jnp.concatenate(reals, axis=1), jnp.concatenate(imags, axis=1)], axis=0
        )
        high, low = split(field)
        field = mm(back_h[...], high) + mm(back_h[...], low) + mm(back_l[...], high)
        for i in range(count):
            z_ref[0, jj + i] = field[:OUTER, lanes[i]]
            z_ref[1, jj + i] = field[OUTER:, lanes[i]]

    for n, (lo, size) in enumerate(chunks):
        bins = pl.ds(lo, size)
        whole = x_ref.at[:, bins]
        pltpu.make_async_copy(whole, whole, frecv.at[n]).wait()
        if size // 2:

            def two(i, carry):
                transform(lo + 2 * i, 2)
                return carry

            lax.fori_loop(0, size // 2, two, 0)
        if size % 2:
            transform(lo + size - 1, 1)
        pltpu.make_async_copy(
            z_ref.at[:, bins, pl.ds(4 * ch, 4)], r_ref.at[:, bins, pl.ds(4 * ch, 4)], brecv.at[n]
        ).start()

        def backward(w, c):
            pltpu.make_async_remote_copy(
                src_ref=z_ref.at[:, bins, pl.ds(4 * c, 4)],
                dst_ref=r_ref.at[:, bins, pl.ds(4 * ch, 4)],
                send_sem=bsend.at[n],
                recv_sem=brecv.at[n],
                device_id=(sec, c),
                device_id_type=MESH,
            ).start()

        each(backward, False)

    for n, (lo, size) in enumerate(chunks):
        bins = pl.ds(lo, size)
        whole = r_ref.at[:, bins]
        pltpu.make_async_copy(whole, whole, brecv.at[n]).wait()
        sent = z_ref.at[:, bins, pl.ds(0, OUTER - 4)]
        pltpu.make_async_copy(sent, sent, bsend.at[n]).wait()
        sent = s_ref.at[:, bins, pl.ds(0, OUTER - 1)]
        pltpu.make_async_copy(sent, sent, fsend.at[n]).wait()


def final_kernel(nb, scal, r_ref, table_h, table_l, out_ref, turned_h, turned_l):
    rows = nb * SHARDS
    f0 = pl.multiple_of(first_bin(scal, nb), ALIGN)
    for block in range(4):
        for part in range(2):
            value = r_ref[part, pl.ds(block, rows, stride=4), :] * 2.0
            high, low = split(value.T)
            turned_h[part, block * INNER : (block + 1) * INNER, :] = high
            turned_l[part, block * INNER : (block + 1) * INNER, :] = low

    def column(n, carry):
        cols = pl.ds(pl.multiple_of(n * 256, 256), 256)
        total = jnp.zeros((4 * INNER, 256), jnp.float32)
        for part in range(2):
            th = table_h[part, pl.ds(f0 + PAD, rows), cols]
            tl = table_l[part, pl.ds(f0 + PAD, rows), cols]
            total = total + mm(turned_h[part], th)
            total = total + mm(turned_l[part], th)
            total = total + mm(turned_h[part], tl)
        out_ref[:, cols] = total
        return carry

    lax.fori_loop(0, SAMPLES // 256, column, 0)


def chunks_of(nb):
    first = (nb + 1) // 2
    first += first % 2 if nb > 2 else 0
    return [(0, first), (first, nb - first)] if nb > first else [(0, nb)]


def branch(nb, scal, strain, taps, weight, table_h, table_l, *waves):
    rows = nb * SHARDS
    wide = rows + 2 * PAD
    smem = pl.BlockSpec(memory_space=SM)
    vmem = pl.BlockSpec(memory_space=VM)
    spectrum = pl.pallas_call(
        functools.partial(front_kernel, nb),
        out_shape=jax.ShapeDtypeStruct((2, nb, SECTIONS * SHARDS, INNER), jnp.float32),
        in_specs=[smem] + [vmem] * 5,
        out_specs=vmem,
        scratch_shapes=[
            VM((2 * INNER, SAMPLES), jnp.float32),
            VM((wide, 2 * INNER), jnp.float32),
            VM((2, wide, 2 * INNER), jnp.float32),
        ],
        compiler_params=pltpu.CompilerParams(vmem_limit_bytes=VMEM_LIMIT),
        name=f"front{nb}",
    )(scal, strain, taps, weight, table_h, table_l)
    chunks = chunks_of(nb)
    count = len(chunks)
    dma = pltpu.SemaphoreType.DMA((count,))
    field = jax.ShapeDtypeStruct((2, nb, OUTER, INNER), jnp.float32)
    passed = pl.pallas_call(
        functools.partial(wave_kernel, nb, chunks),
        out_shape=field,
        in_specs=[smem] + [vmem] * 10,
        out_specs=vmem,
        scratch_shapes=[VM(field.shape, jnp.float32), VM(field.shape, jnp.float32)] + [dma] * 4,
        compiler_params=pltpu.CompilerParams(
            vmem_limit_bytes=VMEM_LIMIT, has_side_effects=True, collective_id=nb
        ),
        name=f"wave{nb}",
    )(scal, spectrum, *waves)
    passed = passed.reshape(2, nb * OUTER, INNER)
    return pl.pallas_call(
        functools.partial(final_kernel, nb),
        out_shape=jax.ShapeDtypeStruct((4 * INNER, SAMPLES), jnp.float32),
        in_specs=[smem] + [vmem] * 3,
        out_specs=vmem,
        scratch_shapes=[VM((2, 4 * INNER, rows), jnp.bfloat16)] * 2,
        compiler_params=pltpu.CompilerParams(vmem_limit_bytes=VMEM_LIMIT),
        name=f"final{nb}",
    )(scal, passed, table_h, table_l)


def per_device(
    strain_rate, fir_taps, gain_code, alive_mask, band_low, band_high, slow_limit, fast_limit
):
    table_h, table_l = time_tables()
    outer, outer_back, inner, inner_back, twist = wave_tables()
    f0 = band_low // ALIGN * ALIGN
    scal = jnp.concatenate([f0, band_low, band_high, slow_limit, fast_limit])
    taps = jnp.pad(fir_taps.astype(jnp.float32)[None, :], ((0, 0), (0, SPAN + OUT - TAPS)))
    weight = (gain_code.astype(jnp.float32) * 0.25 * alive_mask.astype(jnp.float32))[None, :]
    args = (scal, strain_rate, taps, weight, table_h, table_l)
    args = args + outer + outer_back + inner + inner_back + (twist,)
    args = tuple(jnp.asarray(a) for a in args)
    if len(VARIANTS) == 1:
        out = branch(VARIANTS[0], *args)
    else:
        need = (band_high - f0)[0] // SHARDS + 1
        which = sum((need > nb).astype(jnp.int32) for nb in VARIANTS[:-1])
        out = lax.switch(which, [functools.partial(branch, nb) for nb in VARIANTS], *args)
    return out[None]


def solution(mesh):
    placed = (
        P(None, ("sec", "ch"), None),
        P(),
        P(("sec", "ch")),
        P(("sec", "ch")),
        P(),
        P(),
        P(),
        P(),
    )
    return jax.shard_map(
        per_device, mesh=mesh, in_specs=placed, out_specs=P("sec", "ch", None), check_vma=False
    )
```

```python
import functools
import math

import jax
import jax.numpy as jnp
import ml_dtypes
import numpy as np
from jax import lax
from jax.experimental import pallas as pl
from jax.experimental.pallas import tpu as pltpu
from jax.sharding import PartitionSpec as P

TAPS = 64
DECIM = 4
SMOOTH = 4
FLOOR = 0.05
SAMPLES = 1024
BINS = 512
PAD = 16
ALIGN = 16
FIR_OUT = TAPS // DECIM
FIR_ROWS = 256
INNER = 128
OUTER = 256
SECTIONS = 4
SHARDS = 64
TABLE_ROWS = PAD + BINS + PAD
VARIANTS = (2, 4, 6, 8)
VMEM_LIMIT = 48 * 1024 * 1024
MESH = pl.DeviceIdType.MESH
VM = pltpu.VMEM
SM = pltpu.SMEM


def split_np(table):
    table = table.astype(np.float32)
    high = table.astype(ml_dtypes.bfloat16)
    low = (table - high.astype(np.float32)).astype(ml_dtypes.bfloat16)
    return high, low


def split(value):
    high = value.astype(jnp.bfloat16)
    low = (value - high.astype(jnp.float32)).astype(jnp.bfloat16)
    return high, low


def mm(a, b):
    return jnp.dot(a, b, preferred_element_type=jnp.float32)


def time_tables():
    f = np.arange(BINS)[:, None]
    t = np.arange(SAMPLES)[None, :]
    angle = (f * t % SAMPLES) * (2.0 * math.pi / SAMPLES)
    table = np.zeros((2, TABLE_ROWS, SAMPLES))
    table[0, PAD : PAD + BINS] = np.cos(angle) / 32.0
    table[1, PAD : PAD + BINS] = -np.sin(angle) / 32.0
    return split_np(table)


def wave_tables():
    k = np.arange(OUTER)
    angle = (k[:, None] * k[None, :] % OUTER) * (2.0 * math.pi / OUTER)
    c, s = np.cos(angle), np.sin(angle)
    outer = split_np(np.block([[c, s], [-s, c]]))
    outer_back = split_np(np.block([[c, -s], [s, c]]) / (OUTER * INNER))
    j = np.arange(INNER)
    angle = (j[:, None] * j[None, :] % INNER) * (2.0 * math.pi / INNER)
    c, s = np.cos(angle), np.sin(angle)
    inner = split_np(np.block([[c, -s], [s, c]]))
    inner_back = split_np(np.block([[c, s], [-s, c]]))
    angle = k[:, None] * j[None, :] * (2.0 * math.pi / (OUTER * INNER))
    twist = np.stack([np.cos(angle), np.sin(angle)]).astype(np.float32)
    return outer, outer_back, inner, inner_back, twist


def first_bin(scal, nb):
    return jnp.minimum(scal[0], BINS - nb * SHARDS)


def fir_matrix(taps, sections):
    outputs = 2 * FIR_OUT
    width = 2 * FIR_ROWS
    base = jnp.broadcast_to(taps, (outputs, width))
    base = pltpu.roll(base, FIR_ROWS, 1, stride=DECIM * sections, stride_axis=0)[:, :FIR_ROWS]
    column = lax.broadcasted_iota(jnp.int32, (outputs, FIR_ROWS), 1)
    rows = [jnp.where(column % sections == w, base, 0.0) for w in range(sections)]
    return jnp.concatenate(rows, axis=0).astype(jnp.bfloat16)


def decimate(strain, taps, dec):
    matrix = fir_matrix(taps[...], SECTIONS)
    blocks = SAMPLES // FIR_OUT
    outputs = 2 * FIR_OUT

    def add(product, lanes, block, upper):
        for w in range(SECTIONS):
            top = w * outputs + (FIR_OUT if upper else 0)
            where = slice(block * FIR_OUT, (block + 1) * FIR_OUT)
            value = product[top : top + FIR_OUT, lanes]
            if upper:
                dec[w, where, :] = value
            else:
                dec[w, where, :] += value

    for first in range(0, blocks, 2):
        pieces = [strain[n * FIR_ROWS : (n + 1) * FIR_ROWS, :] for n in (first, first + 1)]
        product = mm(matrix, jnp.concatenate(pieces, axis=1))
        for n in (first, first + 1):
            lanes = slice((n - first) * INNER, (n - first + 1) * INNER)
            add(product, lanes, n, True)
            if n:
                add(product, lanes, n - 1, False)
    last = strain.shape[0] - blocks * FIR_ROWS
    product = mm(matrix[:, :last], strain[blocks * FIR_ROWS :, :])
    add(product, slice(0, INNER), blocks - 1, False)


def front_kernel(
    nb, scal, strain, taps, weight, table_h, table_l, s_ref, dec, amp, parts
):
    rows = nb * SHARDS
    wide = rows + 2 * PAD
    f0 = pl.multiple_of(first_bin(scal, nb), ALIGN)
    index = f0 + lax.broadcasted_iota(jnp.int32, (rows, INNER), 0)
    band = ((index >= scal[1]) & (index <= scal[2])).astype(jnp.float32)
    scale = band * weight[...]
    decimate(strain, taps, dec)

    def pair(p, carry):
        high, low = split(jnp.concatenate([dec[2 * p], dec[2 * p + 1]], axis=1))
        for part in range(2):
            th = table_h[part, pl.ds(f0, wide), :]
            tl = table_l[part, pl.ds(f0, wide), :]
            parts[part] = mm(th, high) + mm(th, low) + mm(tl, high)
        real, imag = parts[0], parts[1]
        amp[...] = jnp.sqrt(real * real + imag * imag)
        total = amp[PAD - SMOOTH : PAD - SMOOTH + rows, :]
        for d in range(1, 2 * SMOOTH + 1):
            total = total + amp[PAD - SMOOTH + d : PAD - SMOOTH + d + rows, :]
        smooth = total / (2 * SMOOTH + 1)
        smooth = jnp.maximum(smooth, FLOOR)
        for w in range(2):
            lanes = slice(w * INNER, (w + 1) * INNER)
            factor = scale / smooth[:, lanes]
            start = pl.multiple_of((2 * p + w) * SHARDS, SHARDS)
            for part in range(2):
                value = parts[part, PAD : PAD + rows, lanes] * factor
                s_ref[part, :, pl.ds(start, SHARDS), :] = value.reshape(nb, SHARDS, INNER)
        return carry

    lax.fori_loop(0, SECTIONS // 2, pair, 0)


def wave_kernel(
    nb, chunks, scal, s_ref, outer_h, outer_l, back_h, back_l, in_h, in_l, inb_h, inb_l,
    twist, r_ref, x_ref, z_ref, fsend, frecv, bsend, brecv,
):
    sec = lax.axis_index("sec")
    ch = lax.axis_index("ch")
    y, z, core = ch // 16, (ch // 2) % 8, ch % 2
    me = sec * SHARDS + ch

    def each(action, with_sections):
        first = 16 if with_sections else 4

        def run(dz, dc, start):
            def step(q, carry):
                dx, dy = q // 4, q % 4
                to_ch = ((y + dy) % 4) * 16 + ((z + dz) % 8) * 2 + (core + dc) % 2
                action((sec + dx) % 4, to_ch)
                return carry

            lax.fori_loop(start, first, step, 0)

        for dz in (4, 3, 5, 2, 6, 1, 7):
            for dc in range(2):
                run(dz, dc, 0)
        run(0, 1, 0)
        run(0, 0, 1)

    barrier = pltpu.get_barrier_semaphore()
    each(
        lambda w, b: pl.semaphore_signal(
            barrier, inc=1, device_id=(w, b), device_id_type=MESH
        ),
        True,
    )
    pl.semaphore_wait(barrier, SECTIONS * SHARDS - 1)

    for n, (lo, size) in enumerate(chunks):
        bins = pl.ds(lo, size)
        pltpu.make_async_copy(
            s_ref.at[:, bins, pl.ds(me, 1)], x_ref.at[:, bins, pl.ds(me, 1)], frecv.at[n]
        ).start()

        def forward(w, b):
            pltpu.make_async_remote_copy(
                src_ref=s_ref.at[:, bins, pl.ds(w * SHARDS + b, 1)],
                dst_ref=x_ref.at[:, bins, pl.ds(me, 1)],
                send_sem=fsend.at[n],
                recv_sem=frecv.at[n],
                device_id=(w, b),
                device_id_type=MESH,
            ).start()

        each(forward, True)

    k1 = lax.broadcasted_iota(jnp.int32, (OUTER, INNER), 0)
    k2 = lax.broadcasted_iota(jnp.int32, (OUTER, INNER), 1)
    k = k1 + OUTER * k2
    spacing = jnp.minimum(k, OUTER * INNER - k)
    slow = scal[3] * spacing
    fast = scal[4] * spacing
    rate = 500 * OUTER * INNER // SAMPLES
    cosine, sine = twist[0], twist[1]

    def transform(jj, count):
        lanes = [slice(i * INNER, (i + 1) * INNER) for i in range(count)]
        field = jnp.concatenate(
            [
                jnp.concatenate([x_ref[part, jj + i] for i in range(count)], axis=1)
                for part in range(2)
            ],
            axis=0,
        )
        high, low = split(field)
        field = mm(outer_h[...], high) + mm(outer_h[...], low) + mm(outer_l[...], high)
        stacked = []
        for i in range(count):
            real, imag = field[:OUTER, lanes[i]], field[OUTER:, lanes[i]]
            stacked.append(
                jnp.concatenate(
                    [real * cosine + imag * sine, imag * cosine - real * sine], axis=1
                )
            )
        high, low = split(jnp.concatenate(stacked, axis=0))
        field = mm(high, in_h[...]) + mm(low, in_h[...]) + mm(high, in_l[...])
        masked = []
        for i in range(count):
            reach = (first_bin(scal, nb) + (jj + i) * SHARDS + ch) * rate
            fan = ((slow <= reach) & (reach <= fast)).astype(jnp.float32)
            block = field[i * OUTER : (i + 1) * OUTER]
            masked.append(
                jnp.concatenate([block[:, :INNER] * fan, block[:, INNER:] * fan], axis=1)
            )
        high, low = split(jnp.concatenate(masked, axis=0))
        field = mm(high, inb_h[...]) + mm(low, inb_h[...]) + mm(high, inb_l[...])
        reals, imags = [], []
        for i in range(count):
            block = field[i * OUTER : (i + 1) * OUTER]
            real, imag = block[:, :INNER], block[:, INNER:]
            reals.append(real * cosine - imag * sine)
            imags.append(imag * cosine + real * sine)
        field = jnp.concatenate(
            [jnp.concatenate(reals, axis=1), jnp.concatenate(imags, axis=1)], axis=0
        )
        high, low = split(field)
        field = mm(back_h[...], high) + mm(back_h[...], low) + mm(back_l[...], high)
        for i in range(count):
            z_ref[0, jj + i] = field[:OUTER, lanes[i]]
            z_ref[1, jj + i] = field[OUTER:, lanes[i]]

    for n, (lo, size) in enumerate(chunks):
        bins = pl.ds(lo, size)
        whole = x_ref.at[:, bins]
        pltpu.make_async_copy(whole, whole, frecv.at[n]).wait()
        if size // 2:

            def two(i, carry):
                transform(lo + 2 * i, 2)
                return carry

            lax.fori_loop(0, size // 2, two, 0)
        if size % 2:
            transform(lo + size - 1, 1)
        pltpu.make_async_copy(
            z_ref.at[:, bins, pl.ds(4 * ch, 4)], r_ref.at[:, bins, pl.ds(4 * ch, 4)], brecv.at[n]
        ).start()

        def backward(w, c):
            pltpu.make_async_remote_copy(
                src_ref=z_ref.at[:, bins, pl.ds(4 * c, 4)],
                dst_ref=r_ref.at[:, bins, pl.ds(4 * ch, 4)],
                send_sem=bsend.at[n],
                recv_sem=brecv.at[n],
                device_id=(sec, c),
                device_id_type=MESH,
            ).start()

        each(backward, False)

    for n, (lo, size) in enumerate(chunks):
        bins = pl.ds(lo, size)
        whole = r_ref.at[:, bins]
        pltpu.make_async_copy(whole, whole, brecv.at[n]).wait()
        sent = z_ref.at[:, bins, pl.ds(0, OUTER - 4)]
        pltpu.make_async_copy(sent, sent, bsend.at[n]).wait()
        sent = s_ref.at[:, bins, pl.ds(0, OUTER - 1)]
        pltpu.make_async_copy(sent, sent, fsend.at[n]).wait()


def final_kernel(nb, scal, r_ref, table_h, table_l, out_ref, turned_h, turned_l):
    rows = nb * SHARDS
    f0 = pl.multiple_of(first_bin(scal, nb), ALIGN)
    for block in range(4):
        for part in range(2):
            value = r_ref[part, pl.ds(block, rows, stride=4), :] * 2.0
            high, low = split(value.T)
            turned_h[part, block * INNER : (block + 1) * INNER, :] = high
            turned_l[part, block * INNER : (block + 1) * INNER, :] = low

    def column(n, carry):
        cols = pl.ds(pl.multiple_of(n * 256, 256), 256)
        total = jnp.zeros((4 * INNER, 256), jnp.float32)
        for part in range(2):
            th = table_h[part, pl.ds(f0 + PAD, rows), cols]
            tl = table_l[part, pl.ds(f0 + PAD, rows), cols]
            total = total + mm(turned_h[part], th)
            total = total + mm(turned_l[part], th)
            total = total + mm(turned_h[part], tl)
        out_ref[:, cols] = total
        return carry

    lax.fori_loop(0, SAMPLES // 256, column, 0)


def chunks_of(nb):
    first = (nb + 1) // 2
    first += first % 2 if nb > 2 else 0
    return [(0, first), (first, nb - first)] if nb > first else [(0, nb)]


def branch(nb, scal, strain, taps, weight, table_h, table_l, *waves):
    rows = nb * SHARDS
    wide = rows + 2 * PAD
    smem = pl.BlockSpec(memory_space=SM)
    vmem = pl.BlockSpec(memory_space=VM)
    spectrum = pl.pallas_call(
        functools.partial(front_kernel, nb),
        out_shape=jax.ShapeDtypeStruct((2, nb, SECTIONS * SHARDS, INNER), jnp.float32),
        in_specs=[smem] + [vmem] * 5,
        out_specs=vmem,
        scratch_shapes=[
            VM((SECTIONS, SAMPLES, INNER), jnp.float32),
            VM((wide, 2 * INNER), jnp.float32),
            VM((2, wide, 2 * INNER), jnp.float32),
        ],
        compiler_params=pltpu.CompilerParams(vmem_limit_bytes=VMEM_LIMIT),
        name=f"front{nb}",
    )(scal, strain, taps, weight, table_h, table_l)
    chunks = chunks_of(nb)
    count = len(chunks)
    dma = pltpu.SemaphoreType.DMA((count,))
    field = jax.ShapeDtypeStruct((2, nb, OUTER, INNER), jnp.float32)
    passed = pl.pallas_call(
        functools.partial(wave_kernel, nb, chunks),
        out_shape=field,
        in_specs=[smem] + [vmem] * 10,
        out_specs=vmem,
        scratch_shapes=[VM(field.shape, jnp.float32), VM(field.shape, jnp.float32)] + [dma] * 4,
        compiler_params=pltpu.CompilerParams(
            vmem_limit_bytes=VMEM_LIMIT, has_side_effects=True, collective_id=nb
        ),
        name=f"wave{nb}",
    )(scal, spectrum, *waves)
    passed = passed.reshape(2, nb * OUTER, INNER)
    return pl.pallas_call(
        functools.partial(final_kernel, nb),
        out_shape=jax.ShapeDtypeStruct((4 * INNER, SAMPLES), jnp.float32),
        in_specs=[smem] + [vmem] * 3,
        out_specs=vmem,
        scratch_shapes=[VM((2, 4 * INNER, rows), jnp.bfloat16)] * 2,
        compiler_params=pltpu.CompilerParams(vmem_limit_bytes=VMEM_LIMIT),
        name=f"final{nb}",
    )(scal, passed, table_h, table_l)


def per_device(
    strain_rate, fir_taps, gain_code, alive_mask, band_low, band_high, slow_limit, fast_limit
):
    table_h, table_l = time_tables()
    outer, outer_back, inner, inner_back, twist = wave_tables()
    f0 = band_low // ALIGN * ALIGN
    scal = jnp.concatenate([f0, band_low, band_high, slow_limit, fast_limit])
    taps = jnp.repeat(fir_taps.astype(jnp.float32), SECTIONS)[None, :]
    taps = jnp.pad(taps, ((0, 0), (0, FIR_ROWS)))
    strain = jnp.transpose(strain_rate, (2, 0, 1)).reshape(-1, INNER)
    weight = (gain_code.astype(jnp.float32) * 0.25 * alive_mask.astype(jnp.float32))[None, :]
    args = (scal, strain, taps, weight, table_h, table_l)
    args = args + outer + outer_back + inner + inner_back + (twist,)
    args = tuple(jnp.asarray(a) for a in args)
    if len(VARIANTS) == 1:
        out = branch(VARIANTS[0], *args)
    else:
        need = (band_high - f0)[0] // SHARDS + 1
        which = sum((need > nb).astype(jnp.int32) for nb in VARIANTS[:-1])
        out = lax.switch(which, [functools.partial(branch, nb) for nb in VARIANTS], *args)
    return out[None]


def solution(mesh):
    placed = (
        P(None, ("sec", "ch"), None),
        P(),
        P(("sec", "ch")),
        P(("sec", "ch")),
        P(),
        P(),
        P(),
        P(),
    )
    return jax.shard_map(
        per_device, mesh=mesh, in_specs=placed, out_specs=P("sec", "ch", None), check_vma=False
    )
```
